32 devices in a mesh: shell: 8 (over z, x), blk: 4 (over y, core).
Axes of the slice: x: 2, y: 2, z: 4, core: 2. Of those that a mesh axis runs over, the one named last changes fastest.
Arguments:
- cycle_fourier: bfloat16 [512, 2, 192, 1024], P('shell', None, None, 'blk'), may hold values from -6 to 6
- legendre: bfloat16 [192, 768, 1024], P('shell', None, 'blk'), may hold values from -0.1875 to 0.1875
- azimuth_orders: int32 [192], replicated, may hold values from 0 to 767, as said below
- multipole: int32 [768], P(('shell', 'blk')), may hold values from 0 to 767, each once
- bessel: bfloat16 [768, 512, 512], P(('shell', 'blk')), may hold values from -0.25 to 0.25
- signal_power: float32 [768, 512], P(('shell', 'blk')), may hold values from 0.1 to 10
- noise_power: float32 [768, 512], P(('shell', 'blk')), may hold values from 0.1 to 10
Outputs:
- filtered: bfloat16 [768, 512, 384], P('shell', 'blk')
The draws below stay inside these ranges and needn't reach their ends.
Inputs may be any that keep to these rules, and one draw needn't show every extreme that they name: `azimuth_orders`: distinct orders; 0 and 767 always among them. Each multipole 0 to 767 appears once.
All inputs are finite; a program needn't handle non-finite values.
Results may differ from the reference program's by a relative error of at most 0.017.
Values may be sent and summed in bfloat16 or wider, within the bound.
No kernel may reach another device: no remote copies, remote signals or barrier semaphores. Data moves between devices by JAX's collectives and lax.ppermute only.
A program may use at most 192 MiB of HBM per device.

```python
import math
import jax
import jax.numpy as jnp
from jax import lax

L = 768
CYCLES = 1024
SHELLS = 512
M_COLS = 192
N_BLK = 4


def draw_azimuth_orders(key, part):
    inner = jax.random.permutation(jax.random.fold_in(key, 11), L - 2)[:M_COLS - 2] + 1
    joined = jnp.concatenate([jnp.array([0, L - 1], jnp.int32), inner.astype(jnp.int32)])
    return jax.random.permutation(jax.random.fold_in(key, 12), joined).astype(jnp.int32)


def steps_of(rng, extent, cuts, smallest, top_value):
    factor_of, own = 1.0, jax.random.fold_in(rng, 6)
    for axis_at, shards_of in cuts:
        draws = jnp.exp(jax.random.uniform(jax.random.fold_in(own, axis_at), (shards_of,), jnp.float32, smallest / len(cuts), top_value / len(cuts)))
        factor_of = factor_of * jnp.repeat(draws, extent[axis_at] // shards_of).reshape([-1 if axis == axis_at else 1 for axis in range(len(extent))])
    return factor_of


def noise(own_key, dims, width, reach, shards=(), dtype=jnp.bfloat16):
    result = width * jax.random.normal(own_key, dims, jnp.float32)
    if shards:
        result = result * steps_of(own_key, dims, shards, -0.22, 0.18)
    return jnp.clip(result, -reach, reach).astype(dtype)


def setup_inputs(seed: int = 0) -> dict:
    key_list = jax.random.split(jax.random.key(seed), 8)
    return {
        "cycle_fourier": noise(key_list[0], (SHELLS, 2, M_COLS, CYCLES), 1.0, 6.0, ((0, 8), (3, 4))),
        "legendre": noise(key_list[1], (M_COLS, L, CYCLES), CYCLES ** -0.5, 0.1875, ((0, 8), (2, 4))),
        "azimuth_orders": draw_azimuth_orders(jax.random.fold_in(key_list[7], 71), 0),
        "multipole": jax.random.permutation(key_list[3], L).astype(jnp.int32),
        "bessel": noise(key_list[4], (L, SHELLS, SHELLS), SHELLS ** -0.5, 0.25, ((0, 32),)),
        "signal_power": jnp.clip(jnp.exp(math.log(10.0) - 4.6051702 * jax.random.uniform(key_list[5], (L, SHELLS), jnp.float32) ** steps_of(key_list[5], (L, SHELLS), ((0, 32),), -0.2, 0.2)), 0.1, 10.0),
        "noise_power": jnp.clip(jnp.exp(math.log(10.0) - 4.6051702 * jax.random.uniform(key_list[6], (L, SHELLS), jnp.float32) ** steps_of(key_list[6], (L, SHELLS), ((0, 32),), -0.2, 0.2)), 0.1, 10.0),
    }


def reference(cycle_fourier, legendre, azimuth_orders, multipole, bessel, signal_power, noise_power):
    cycle_span = CYCLES // N_BLK
    accumulated = jnp.zeros((L, M_COLS, 2, SHELLS), jnp.float32)
    for blocks in range(N_BLK):
        fields = cycle_fourier[:, :, :, blocks * cycle_span:(blocks + 1) * cycle_span].astype(jnp.float32)
        tables = legendre[:, :, blocks * cycle_span:(blocks + 1) * cycle_span].astype(jnp.float32)
        partial_value = jnp.einsum("jir,scjr->ijcs", tables, fields).astype(jnp.bfloat16)
        partial_value = lax.optimization_barrier(partial_value)
        accumulated = accumulated + partial_value.astype(jnp.float32)
    allowed = multipole[:, None] >= azimuth_orders[None, :]
    coeffs = jnp.where(allowed[:, :, None, None], accumulated, 0.0).astype(jnp.bfloat16)
    bessel_wide = bessel.astype(jnp.float32)
    forward = jnp.einsum("iks,ijcs->ijck", bessel_wide, coeffs.astype(jnp.float32))
    wiener = signal_power / (signal_power + noise_power)
    scaled = (forward * wiener[:, None, None, :]).astype(jnp.bfloat16)
    filtered = jnp.einsum("iks,ijck->isjc", bessel_wide, scaled.astype(jnp.float32))
    return filtered.reshape(L, SHELLS, 2 * M_COLS).astype(jnp.bfloat16)
```

```python
import functools
import math

import jax
import jax.numpy as jnp
from jax import lax
from jax.experimental import pallas as pl
from jax.experimental.pallas import tpu as pltpu
from jax.sharding import PartitionSpec as P

BOTH = ("shell", "blk")
VMEM = 48 * 1024 * 1024


def exchange(blocks, axis, size):
    return [blocks[0]] + [
        lax.ppermute(blocks[d], axis, [(i, i ^ d) for i in range(size)]) for d in range(1, size)
    ]


def legendre_kernel(groups, spread, parts, me, own, *refs):
    tables, fields, out = refs[: groups - 1], refs[groups - 1], refs[groups]
    lhs = jnp.concatenate([own[0]] + [t[0] for t in tables], axis=1)
    shells = fields.shape[0]
    height = fields.shape[3] // parts
    for c in range(parts):
        rows = [
            jnp.concatenate(
                [fields[s, me[0] ^ d, 0, c * height : (c + 1) * height] for d in range(groups)], axis=1
            )
            for s in range(shells)
        ]
        rhs = jnp.concatenate(rows, axis=0)
        total = lax.dot_general(lhs, rhs, (((1,), (1,)), ((), ())), preferred_element_type=jnp.float32)
        width = shells * height
        out[:, c * width : (c + 1) * width] = total.astype(out.dtype)


def legendre_transform(me, own, tables, fields, first, count, per_device, spread, parts):
    shells, groups, _, height, cycles = fields.shape
    rows = own.shape[1]
    at, offset = first
    width = shells * height
    grid_spec = pltpu.PrefetchScalarGridSpec(
        num_scalar_prefetch=1,
        grid=(count,),
        in_specs=[
            pl.BlockSpec((1, rows, cycles), lambda u, me: (me[0] // spread * per_device + at + offset + u, 0, 0))
        ]
        + [pl.BlockSpec((1, rows, cycles), lambda u, me: (at + offset + u, 0, 0))] * (groups - 1)
        + [pl.BlockSpec((shells, groups, 1, height, cycles), lambda u, me: (0, 0, offset + u, 0, 0))],
        out_specs=pl.BlockSpec((rows, width), lambda u, me: (0, u)),
    )
    flops = 2 * count * rows * width * cycles * groups
    return pl.pallas_call(
        functools.partial(legendre_kernel, groups, spread, parts),
        grid_spec=grid_spec,
        out_shape=jax.ShapeDtypeStruct((rows, count * width), jnp.bfloat16),
        compiler_params=pltpu.CompilerParams(vmem_limit_bytes=VMEM),
        cost_estimate=pl.CostEstimate(
            flops=flops, bytes_accessed=2 * count * (rows * width + groups * cycles * (rows + width)), transcendentals=0
        ),
        name="legendre",
    )(me, own, *tables, fields)


def radial_kernel(groups, step, scalars, coeffs, orders, bessel, signal, noise, *refs):
    outs, held = refs[:groups], refs[groups]
    first = pl.program_id(0) * step
    shells, width = bessel.shape[2], held.shape[2]
    pieces = coeffs.shape[2] // shells
    for t in range(step):
        row = jnp.concatenate([coeffs[:, t, n * shells : (n + 1) * shells] for n in range(pieces)], axis=0)
        allowed = scalars[1 + first + t] >= orders[...]
        masked = jnp.where(allowed, row, jnp.zeros((), row.dtype))
        forward = lax.dot_general(bessel[t], masked, (((1,), (1,)), ((), ())), preferred_element_type=jnp.float32)
        wiener = signal[t] / (signal[t] + noise[t])
        scaled = (forward.T * wiener).astype(jnp.bfloat16)
        back = jnp.dot(scaled, bessel[t], preferred_element_type=jnp.float32).astype(jnp.bfloat16)
        for b in range(groups):
            held[b] = back[:, b * width : (b + 1) * width]
        for d in range(groups):
            outs[d][t] = held[scalars[0] ^ d]


def radial_transform(scalars, coeffs, orders, bessel, signal, noise, groups):
    devices, rows, _ = coeffs.shape
    waves, shells = bessel.shape[1:]
    columns = orders.shape[0]
    width = shells // groups
    step = 8 if rows % 8 == 0 else rows
    grid_spec = pltpu.PrefetchScalarGridSpec(
        num_scalar_prefetch=1,
        grid=(rows // step,),
        in_specs=[
            pl.BlockSpec((devices, step, coeffs.shape[2]), lambda t, s: (0, t, 0)),
            pl.BlockSpec((columns, 1), lambda t, s: (0, 0)),
            pl.BlockSpec((step, waves, shells), lambda t, s: (t, 0, 0)),
            pl.BlockSpec((step, 1, waves), lambda t, s: (t, 0, 0)),
            pl.BlockSpec((step, 1, waves), lambda t, s: (t, 0, 0)),
        ],
        out_specs=[pl.BlockSpec((step, columns, width), lambda t, s: (t, 0, 0))] * groups,
        scratch_shapes=[pltpu.VMEM((groups, columns, width), jnp.bfloat16)],
    )
    return pl.pallas_call(
        functools.partial(radial_kernel, groups, step),
        grid_spec=grid_spec,
        out_shape=[jax.ShapeDtypeStruct((rows, columns, width), jnp.bfloat16)] * groups,
        compiler_params=pltpu.CompilerParams(vmem_limit_bytes=VMEM),
        cost_estimate=pl.CostEstimate(
            flops=4 * rows * columns * waves * shells,
            bytes_accessed=2 * rows * (waves * shells + 2 * columns * shells),
            transcendentals=0,
        ),
        name="radial",
    )(scalars, coeffs, orders, bessel, signal, noise)


def order_kernel(pieces, step, me, *refs):
    ins, place, out = refs[:pieces], refs[pieces], refs[-1]
    turned = [
        jnp.concatenate([p[t].astype(jnp.float32) for p in ins], axis=0).T.astype(jnp.bfloat16) for t in range(step)
    ]
    mixed = jnp.dot(jnp.concatenate(turned, axis=0), place[...], preferred_element_type=jnp.float32)
    width = out.shape[1]
    for t in range(step):
        out[t] = mixed[t * width : (t + 1) * width].astype(out.dtype)


def put_in_order(me, pieces, place, distance, so_far, groups):
    rows, _, width = pieces[0].shape
    columns = place.shape[0]
    step = math.gcd(rows, 8)
    specs = [pl.BlockSpec((step, p.shape[1], width), lambda t, me: (t, 0, 0)) for p in pieces]
    specs.append(pl.BlockSpec((columns, columns), lambda t, me: (0, 0)))
    operands = list(pieces) + [place]
    aliases = {}
    if so_far is not None:
        specs.append(pl.BlockSpec(memory_space=pl.ANY))
        operands.append(so_far)
        aliases = {len(operands): 0}
    grid_spec = pltpu.PrefetchScalarGridSpec(
        num_scalar_prefetch=1,
        grid=(rows // step,),
        in_specs=specs,
        out_specs=pl.BlockSpec((step, width, columns), lambda t, me: ((me[0] ^ distance) * (rows // step) + t, 0, 0)),
    )
    return pl.pallas_call(
        functools.partial(order_kernel, len(pieces), step),
        grid_spec=grid_spec,
        out_shape=jax.ShapeDtypeStruct((groups * rows, width, columns), jnp.bfloat16),
        input_output_aliases=aliases,
        compiler_params=pltpu.CompilerParams(vmem_limit_bytes=VMEM),
        cost_estimate=pl.CostEstimate(
            flops=2 * rows * width * columns * columns, bytes_accessed=4 * rows * width * columns, transcendentals=0
        ),
        name="in_order",
    )(me, *operands)


def body(cycle_fourier, legendre, azimuth_orders, multipole, bessel, signal_power, noise_power):
    shells, groups = lax.axis_size("shell"), lax.axis_size("blk")
    devices = shells * groups
    here, complex_parts, orders, cycles = cycle_fourier.shape
    local_orders, rows, _ = legendre.shape
    local_rows = multipole.shape[0]
    sharers = math.gcd(local_orders, groups)
    spread = groups // sharers
    per_device = local_orders // sharers
    parts = complex_parts // spread
    all_shells = shells * here
    me = lax.axis_index("blk").astype(jnp.int32)
    me1 = me.reshape(1)

    mine = legendre.reshape(sharers, per_device, rows, cycles)
    tables = exchange(
        [None] + [lax.dynamic_index_in_dim(mine, (me ^ d) // spread, 0, False) for d in range(1, groups)], "blk", groups
    )[1:]

    half = max(per_device // 2, 1)
    spans = [(0, half), (half, per_device)]
    view = cycle_fourier.reshape(here, spread, parts, shells, sharers, per_device, cycles)

    def send_fields(lo, hi):
        packed = view[..., lo:hi, :].transpose(3, 4, 1, 5, 2, 0, 6).reshape(devices, hi - lo, parts * here, cycles)
        return packed

    def move(x):
        return lax.all_to_all(x, BOTH, split_axis=0, concat_axis=0, tiled=True)

    def received(x):
        return x.reshape(shells, groups, x.shape[1], parts * here, cycles)

    fields = [received(move(send_fields(*spans[0])))]
    late_half, *tables = lax.optimization_barrier((send_fields(*spans[1]), *tables))
    fields.append(received(move(late_half)))

    chunks = [(0, 0, half)]
    rest = per_device - half
    late = max(rest // 3, 1)
    chunks += [(1, 0, rest - late), (1, rest - late, rest)]
    chunks = [c for c in chunks if c[2] > c[1]]
    signal = signal_power[:, None, :]
    noise = noise_power[:, None, :]
    scalars = jnp.concatenate([me1, multipole])
    order_view = azimuth_orders.reshape(shells, sharers, 1, per_device, 1)
    column_view = jnp.arange(orders * complex_parts).reshape(shells, sharers, per_device, spread, parts)

    def coefficients(chunk):
        which, lo, hi = chunk
        return legendre_transform(
            me1, legendre, tables, fields[which], (spans[which][0], lo), hi - lo, per_device, spread, parts
        ).reshape(devices, local_rows, -1)

    def filtered(chunk, y):
        which, lo, hi = chunk
        first, count = spans[which][0] + lo, hi - lo
        limit = jnp.broadcast_to(
            order_view[:, :, :, first : first + count], (shells, sharers, spread, count, parts)
        ).transpose(3, 4, 0, 1, 2)
        columns = column_view[:, :, first : first + count].transpose(2, 4, 0, 1, 3)
        outs = radial_transform(scalars, y, limit.reshape(-1, 1), bessel, signal, noise, groups)
        return outs, columns.reshape(-1)

    gathered, places = [], []
    first, fields[1] = lax.optimization_barrier((coefficients(chunks[0]), fields[1]))
    arrived = move(first)
    for k in range(len(chunks)):
        if k + 1 < len(chunks):
            following = coefficients(chunks[k + 1])
            if k > 0:
                following, gathered[k - 1] = lax.optimization_barrier((following, gathered[k - 1]))
            following, arrived = lax.optimization_barrier((following, arrived))
            coming = move(following)
        outs, columns = filtered(chunks[k], arrived)
        gathered.append(outs)
        places.append(columns)
        if k + 1 < len(chunks):
            arrived = coming
    gathered = [exchange(outs, "blk", groups) for outs in gathered]
    place = (jnp.concatenate(places)[:, None] == jnp.arange(orders * complex_parts)[None, :]).astype(jnp.bfloat16)
    out = None
    for d in range(groups):
        out = put_in_order(me1, [g[d] for g in gathered], place, d, out, groups)
    return out


def solution(mesh):
    return jax.shard_map(
        body,
        mesh=mesh,
        in_specs=(
            P("shell", None, None, "blk"),
            P("shell", None, "blk"),
            P(),
            P(("shell", "blk")),
            P(("shell", "blk"), None, None),
            P(("shell", "blk"), None),
            P(("shell", "blk"), None),
        ),
        out_specs=P("shell", "blk", None),
        check_vma=False,
    )
```

```python
import functools
import math

import jax
import jax.numpy as jnp
from jax import lax
from jax.experimental import pallas as pl
from jax.experimental.pallas import tpu as pltpu
from jax.sharding import PartitionSpec as P

BOTH = ("shell", "blk")
FIELD_SHARES = (0, 3, 6)
SHARES = (0, 1, 3, 5, 6)
VMEM = 48 * 1024 * 1024


def exchange(blocks, axis, size):
    return [blocks[0]] + [
        lax.ppermute(blocks[d], axis, [(i, i ^ d) for i in range(size)]) for d in range(1, size)
    ]


def legendre_kernel(groups, spread, parts, me, own, *refs):
    tables, fields, out = refs[: groups - 1], refs[groups - 1], refs[groups]
    lhs = jnp.concatenate([own[0]] + [t[0] for t in tables], axis=1)
    shells = fields.shape[0]
    height = fields.shape[3] // parts
    for c in range(parts):
        rows = [
            jnp.concatenate(
                [fields[s, me[0] ^ d, 0, c * height : (c + 1) * height] for d in range(groups)], axis=1
            )
            for s in range(shells)
        ]
        rhs = jnp.concatenate(rows, axis=0)
        total = lax.dot_general(lhs, rhs, (((1,), (1,)), ((), ())), preferred_element_type=jnp.float32)
        width = shells * height
        out[:, c * width : (c + 1) * width] = total.astype(out.dtype)


def legendre_transform(me, own, tables, fields, first, count, per_device, spread, parts):
    shells, groups, _, height, cycles = fields.shape
    rows = own.shape[1]
    at, offset = first
    width = shells * height
    grid_spec = pltpu.PrefetchScalarGridSpec(
        num_scalar_prefetch=1,
        grid=(count,),
        in_specs=[
            pl.BlockSpec((1, rows, cycles), lambda u, me: (me[0] // spread * per_device + at + offset + u, 0, 0))
        ]
        + [pl.BlockSpec((1, rows, cycles), lambda u, me: (offset + u, 0, 0))] * (groups - 1)
        + [pl.BlockSpec((shells, groups, 1, height, cycles), lambda u, me: (0, 0, offset + u, 0, 0))],
        out_specs=pl.BlockSpec((rows, width), lambda u, me: (0, u)),
    )
    flops = 2 * count * rows * width * cycles * groups
    return pl.pallas_call(
        functools.partial(legendre_kernel, groups, spread, parts),
        grid_spec=grid_spec,
        out_shape=jax.ShapeDtypeStruct((rows, count * width), jnp.bfloat16),
        compiler_params=pltpu.CompilerParams(vmem_limit_bytes=VMEM),
        cost_estimate=pl.CostEstimate(
            flops=flops, bytes_accessed=2 * count * (rows * width + groups * cycles * (rows + width)), transcendentals=0
        ),
        name="legendre",
    )(me, own, *tables, fields)


def filter_kernel(bessel, signal, noise, out):
    for t in range(bessel.shape[0]):
        wiener = signal[t] / (signal[t] + noise[t])
        turned = (bessel[t].astype(jnp.float32).T * wiener).astype(jnp.bfloat16)
        out[t] = jnp.dot(turned, bessel[t], preferred_element_type=jnp.float32).astype(out.dtype)


def radial_filter(bessel, signal, noise):
    rows, waves, shells = bessel.shape
    return pl.pallas_call(
        filter_kernel,
        grid=(rows,),
        in_specs=[
            pl.BlockSpec((1, waves, shells), lambda t: (t, 0, 0)),
            pl.BlockSpec((1, 1, waves), lambda t: (t, 0, 0)),
            pl.BlockSpec((1, 1, waves), lambda t: (t, 0, 0)),
        ],
        out_specs=pl.BlockSpec((1, shells, shells), lambda t: (t, 0, 0)),
        out_shape=jax.ShapeDtypeStruct((rows, shells, shells), jnp.bfloat16),
        compiler_params=pltpu.CompilerParams(vmem_limit_bytes=VMEM),
        cost_estimate=pl.CostEstimate(
            flops=2 * rows * waves * shells * shells, bytes_accessed=4 * rows * shells * waves, transcendentals=0
        ),
        name="radial_filter",
    )(bessel, signal, noise)


def radial_kernel(groups, step, at, coeffs, orders, response, *refs):
    outs, held = refs[:groups], refs[groups]
    first = pl.program_id(0) * step
    length, width = response.shape[1], held.shape[3]
    pieces = coeffs.shape[2] // length
    for t in range(step):
        row = jnp.concatenate([coeffs[:, t, n * length : (n + 1) * length] for n in range(pieces)], axis=0)
        allowed = at[1 + first + t] >= orders[...]
        masked = jnp.where(allowed, row, jnp.zeros((), row.dtype))
        back = jnp.dot(masked, response[t], preferred_element_type=jnp.float32).astype(jnp.bfloat16)
        for b in range(groups):
            held[t, b] = back[:, b * width : (b + 1) * width]
        for d in range(groups):
            outs[d][t] = held[t, at[0] ^ d]


def radial_transform(at, coeffs, orders, response, groups):
    senders, rows, lanes = coeffs.shape
    length = response.shape[1]
    columns = orders.shape[0]
    width = length // groups
    step = 8 if rows % 8 == 0 else rows
    grid_spec = pltpu.PrefetchScalarGridSpec(
        num_scalar_prefetch=1,
        grid=(rows // step,),
        in_specs=[
            pl.BlockSpec((senders, step, lanes), lambda t, at: (0, t, 0)),
            pl.BlockSpec((columns, 1), lambda t, at: (0, 0)),
            pl.BlockSpec((step, length, length), lambda t, at: (t, 0, 0)),
        ],
        out_specs=[pl.BlockSpec((step, columns, width), lambda t, at: (t, 0, 0))] * groups,
        scratch_shapes=[pltpu.VMEM((step, groups, columns, width), jnp.bfloat16)],
    )
    return pl.pallas_call(
        functools.partial(radial_kernel, groups, step),
        grid_spec=grid_spec,
        out_shape=[jax.ShapeDtypeStruct((rows, columns, width), jnp.bfloat16)] * groups,
        compiler_params=pltpu.CompilerParams(vmem_limit_bytes=VMEM),
        cost_estimate=pl.CostEstimate(
            flops=2 * rows * columns * length * length,
            bytes_accessed=2 * rows * (length * length + 2 * columns * length),
            transcendentals=0,
        ),
        name="radial",
    )(at, coeffs, orders, response)


def order_kernel(pieces, step, me, *refs):
    ins, place, out = refs[:pieces], refs[pieces], refs[-1]
    turned = [
        jnp.concatenate([p[t].astype(jnp.float32) for p in ins], axis=0).T.astype(jnp.bfloat16) for t in range(step)
    ]
    mixed = jnp.dot(jnp.concatenate(turned, axis=0), place[...], preferred_element_type=jnp.float32)
    width = out.shape[1]
    for t in range(step):
        out[t] = mixed[t * width : (t + 1) * width].astype(out.dtype)


def put_in_order(me, pieces, place, distance, so_far, groups):
    rows, _, width = pieces[0].shape
    columns = place.shape[0]
    step = math.gcd(rows, 8)
    specs = [pl.BlockSpec((step, p.shape[1], width), lambda t, me: (t, 0, 0)) for p in pieces]
    specs.append(pl.BlockSpec((columns, columns), lambda t, me: (0, 0)))
    operands = list(pieces) + [place]
    aliases = {}
    if so_far is not None:
        specs.append(pl.BlockSpec(memory_space=pl.ANY))
        operands.append(so_far)
        aliases = {len(operands): 0}
    grid_spec = pltpu.PrefetchScalarGridSpec(
        num_scalar_prefetch=1,
        grid=(rows // step,),
        in_specs=specs,
        out_specs=pl.BlockSpec((step, width, columns), lambda t, me: ((me[0] ^ distance) * (rows // step) + t, 0, 0)),
    )
    return pl.pallas_call(
        functools.partial(order_kernel, len(pieces), step),
        grid_spec=grid_spec,
        out_shape=jax.ShapeDtypeStruct((groups * rows, width, columns), jnp.bfloat16),
        input_output_aliases=aliases,
        compiler_params=pltpu.CompilerParams(vmem_limit_bytes=VMEM),
        cost_estimate=pl.CostEstimate(
            flops=2 * rows * width * columns * columns, bytes_accessed=4 * rows * width * columns, transcendentals=0
        ),
        name="in_order",
    )(me, *operands)


def body(cycle_fourier, legendre, azimuth_orders, multipole, bessel, signal_power, noise_power):
    shells, groups = lax.axis_size("shell"), lax.axis_size("blk")
    devices = shells * groups
    here, complex_parts, orders, cycles = cycle_fourier.shape
    local_orders, rows, _ = legendre.shape
    local_rows = multipole.shape[0]
    sharers = math.gcd(local_orders, groups)
    spread = groups // sharers
    per_device = local_orders // sharers
    parts = complex_parts // spread
    me = lax.axis_index("blk").astype(jnp.int32)
    at = jnp.concatenate([me.reshape(1), multipole])

    cuts = [round(per_device * share / FIELD_SHARES[-1]) for share in FIELD_SHARES]
    spans = [(lo, hi) for lo, hi in zip(cuts, cuts[1:]) if hi > lo]
    cuts = [round(per_device * share / SHARES[-1]) for share in SHARES]
    chunks = [(lo, hi) for lo, hi in zip(cuts, cuts[1:]) if hi > lo]
    view = cycle_fourier.reshape(here, spread, parts, shells, sharers, per_device, cycles)

    def packed(span):
        lo, hi = span
        return view[..., lo:hi, :].transpose(3, 4, 1, 5, 2, 0, 6).reshape(devices, hi - lo, parts * here, cycles)

    def move(x):
        return lax.all_to_all(x, BOTH, split_axis=0, concat_axis=0, tiled=True)

    def send_tables(span, earlier):
        lo, hi = span
        blocks = [
            lax.dynamic_slice_in_dim(legendre, (me ^ d) // spread * per_device + lo, hi - lo, 0) for d in range(1, groups)
        ]
        return exchange([None] + after(earlier, blocks), "blk", groups)[1:]

    def after(earlier, later):
        return lax.optimization_barrier((earlier, later))[1]

    order_view = azimuth_orders.reshape(shells, sharers, 1, per_device, 1)
    column_view = jnp.arange(orders * complex_parts).reshape(shells, sharers, per_device, spread, parts)
    limits, places = [], []
    for lo, hi in chunks:
        limit = jnp.broadcast_to(order_view[:, :, :, lo:hi], (shells, sharers, spread, hi - lo, parts))
        limits.append(limit.transpose(3, 4, 0, 1, 2).reshape(-1, 1))
        places.append(column_view[:, :, lo:hi].transpose(2, 4, 0, 1, 3).reshape(-1))
    place = (jnp.concatenate(places)[:, None] == jnp.arange(orders * complex_parts)[None, :]).astype(jnp.bfloat16)
    response = radial_filter(bessel, signal_power[:, None, :], noise_power[:, None, :])

    fields, tables = [], []
    earlier = ()
    for k, span in enumerate(spans):
        fields.append(move(after(earlier, packed(span))))
        tables.append(send_tables(span, earlier))
        earlier = (fields[k], tables[k])
        if k == 0:
            earlier, (response, limits, place) = lax.optimization_barrier((earlier, (response, limits, place)))

    def coefficients(chunk):
        lo, hi = chunk
        which = max(i for i, span in enumerate(spans) if span[0] <= lo)
        start = spans[which][0]
        source = fields[which].reshape(shells, groups, *fields[which].shape[1:])
        sent = legendre_transform(
            at, legendre, tables[which], source, (start, lo - start), hi - lo, per_device, spread, parts
        )
        return sent.reshape(devices, local_rows, -1)

    count = len(chunks)
    sent = [coefficients(c) for c in chunks]
    early = [k for k, c in enumerate(chunks) if c[0] < spans[0][1]]
    outs, gathered = [], []
    coming = move(after(([sent[k] for k in early], fields[-1], tables), sent[0]))
    for k in range(count):
        arrived = coming
        if k + 1 < count:
            before = [arrived, sent]
            if k >= 1:
                before += [gathered[k - 1]]
            coming = move(after(before, sent[k + 1]))
        elif k >= 1:
            arrived = after((outs[k - 1], gathered[: k - 1]), arrived)
        outs.append(radial_transform(at, arrived, limits[k], response, groups))
        gathered.append(exchange(outs[k], "blk", groups))

    out = None
    for d in range(groups):
        out = put_in_order(at, [g[d] for g in gathered], place, d, out, groups)
    return out


def solution(mesh):
    return jax.shard_map(
        body,
        mesh=mesh,
        in_specs=(
            P("shell", None, None, "blk"),
            P("shell", None, "blk"),
            P(),
            P(("shell", "blk")),
            P(("shell", "blk"), None, None),
            P(("shell", "blk"), None),
            P(("shell", "blk"), None),
        ),
        out_specs=P("shell", "blk", None),
        check_vma=False,
    )
```

```python
import functools
import math

import jax
import jax.numpy as jnp
import numpy as np
from jax import lax
from jax.experimental import pallas as pl
from jax.experimental.pallas import tpu as pltpu
from jax.sharding import Mesh
from jax.sharding import PartitionSpec as P

LANES = 128
HALF = 8
NEAR = ("x", "blk")
SHELL = ("far", "x")
ALL = ("far", "x", "blk")
FIELD_SHARES = (0, 3, 6)
SHARES = (0, 1, 3, 5, 6)
VMEM = 48 * 1024 * 1024


def exchange(blocks, axis, size):
    return [blocks[0]] + [
        lax.ppermute(blocks[d], axis, [(i, i ^ d) for i in range(size)]) for d in range(1, size)
    ]


def legendre_kernel(groups, parts, by_distance, at, own, *refs):
    tables, fields, out = refs[: groups - 1], refs[groups - 1], refs[groups]
    lhs = jnp.concatenate([own[0]] + [t[0] for t in tables], axis=1)
    shells = fields.shape[0]
    height = fields.shape[3] // parts
    near, far, local_rows, _ = out.shape
    width = shells * height
    for c in range(parts):
        rows = [
            jnp.concatenate(
                [fields[s, at[0] ^ d, 0, c * height : (c + 1) * height] for d in range(groups)], axis=1
            )
            for s in range(shells)
        ]
        rhs = jnp.concatenate(rows, axis=0)
        total = lax.dot_general(lhs, rhs, (((1,), (1,)), ((), ())), preferred_element_type=jnp.float32)
        for i in range(far * near):
            device = i % near
            piece = total[i * local_rows : (i + 1) * local_rows].astype(out.dtype)
            out[device ^ at[1] if by_distance else device, i // near, :, c * width : (c + 1) * width] = piece


def legendre_transform(at, own, tables, fields, first, count, per_device, spread, parts, near, by_distance):
    shells, groups, _, height, cycles = fields.shape
    rows = own.shape[1]
    start, offset = first
    width = shells * height
    far = at_far(shells, groups, near)
    local_rows = rows // (near * far)
    grid_spec = pltpu.PrefetchScalarGridSpec(
        num_scalar_prefetch=1,
        grid=(count,),
        in_specs=[
            pl.BlockSpec((1, rows, cycles), lambda u, at: (at[0] // spread * per_device + start + offset + u, 0, 0))
        ]
        + [pl.BlockSpec((1, rows, cycles), lambda u, at: (offset + u, 0, 0))] * (groups - 1)
        + [pl.BlockSpec((shells, groups, 1, height, cycles), lambda u, at: (0, 0, offset + u, 0, 0))],
        out_specs=pl.BlockSpec((near, far, local_rows, width), lambda u, at: (0, 0, 0, u)),
    )
    flops = 2 * count * rows * width * cycles * groups
    return pl.pallas_call(
        functools.partial(legendre_kernel, groups, parts, by_distance),
        grid_spec=grid_spec,
        out_shape=jax.ShapeDtypeStruct((near, far, local_rows, count * width), jnp.bfloat16),
        compiler_params=pltpu.CompilerParams(vmem_limit_bytes=VMEM),
        cost_estimate=pl.CostEstimate(
            flops=flops, bytes_accessed=2 * count * (rows * width + groups * cycles * (rows + width)), transcendentals=0
        ),
        name="legendre",
    )(at, own, *tables, fields)


def at_far(shells, groups, near):
    return shells * groups // near


def regroup_kernel(count, at, *refs):
    ins, outs = refs[:count], refs[count:]
    for e, out in enumerate(outs):
        for d in range(count):
            out[at[1] ^ d] = ins[d][at[2] ^ e]


def regroup(at, blocks):
    near = len(blocks)
    far, rows, columns = blocks[0].shape
    lanes = columns // 2 if columns % (2 * LANES) == 0 else columns
    specs = [pl.BlockSpec((far, rows, lanes), lambda t, at: (0, 0, t))] * near
    return pl.pallas_call(
        functools.partial(regroup_kernel, len(blocks)),
        grid_spec=pltpu.PrefetchScalarGridSpec(
            num_scalar_prefetch=1,
            grid=(columns // lanes,),
            in_specs=specs,
            out_specs=[pl.BlockSpec((near, rows, lanes), lambda t, at: (0, 0, t))] * far,
        ),
        out_shape=[jax.ShapeDtypeStruct((near, rows, columns), jnp.bfloat16)] * far,
        compiler_params=pltpu.CompilerParams(vmem_limit_bytes=VMEM),
        cost_estimate=pl.CostEstimate(flops=0, bytes_accessed=4 * near * far * rows * columns, transcendentals=0),
        name="regroup",
    )(at, *blocks)


def filter_kernel(groups, at, bessel, signal, noise, out, held):
    for t in range(bessel.shape[0]):
        wiener = signal[t] / (signal[t] + noise[t])
        turned = (bessel[t].astype(jnp.float32).T * wiener).astype(jnp.bfloat16)
        response = jnp.dot(turned, bessel[t], preferred_element_type=jnp.float32).astype(out.dtype)
        width = response.shape[0] // groups
        for b in range(groups):
            held[b] = response[b * width : (b + 1) * width]
        for d in range(groups):
            out[t, d * width : (d + 1) * width] = held[at[0] ^ d]


def radial_filter(at, bessel, signal, noise, groups):
    rows, waves, shells = bessel.shape
    return pl.pallas_call(
        functools.partial(filter_kernel, groups),
        grid_spec=pltpu.PrefetchScalarGridSpec(
            num_scalar_prefetch=1,
            grid=(rows,),
            in_specs=[
                pl.BlockSpec((1, waves, shells), lambda t, at: (t, 0, 0)),
                pl.BlockSpec((1, 1, waves), lambda t, at: (t, 0, 0)),
                pl.BlockSpec((1, 1, waves), lambda t, at: (t, 0, 0)),
            ],
            out_specs=pl.BlockSpec((1, shells, shells), lambda t, at: (t, 0, 0)),
            scratch_shapes=[pltpu.VMEM((groups, shells // groups, shells), jnp.bfloat16)],
        ),
        out_shape=jax.ShapeDtypeStruct((rows, shells, shells), jnp.bfloat16),
        compiler_params=pltpu.CompilerParams(vmem_limit_bytes=VMEM),
        cost_estimate=pl.CostEstimate(
            flops=2 * rows * waves * shells * shells, bytes_accessed=4 * rows * shells * waves, transcendentals=0
        ),
        name="radial_filter",
    )(at, bessel, signal, noise)


def radial_kernel(groups, far, step, slices, at, *refs):
    ins, orders, responses = refs[:far], refs[far], refs[far + 1 : far + 1 + slices]
    outs, coeffs = refs[far + 1 + slices : -1], refs[-1]
    near = ins[0].shape[0]
    if far == 1:
        coeffs = ins[0]
    else:
        for e in range(far):
            coeffs[pl.ds((at[2] ^ e) * near, near)] = ins[e][...]
    first = pl.program_id(0) * step
    length = responses[0].shape[1]
    width = length // groups
    columns = orders.shape[0]
    fold = outs[0].shape[2] // columns
    senders = near * far
    pieces = coeffs.shape[2] // length
    if step % HALF == 0:
        size = senders * step
        to = lax.broadcasted_iota(jnp.int32, (size, size), 0)
        source = lax.broadcasted_iota(jnp.int32, (size, size), 1)
        pick = jnp.where(source == to % senders * step + to // senders, 1.0, 0.0).astype(coeffs.dtype)
        flat = coeffs[...].reshape(size, coeffs.shape[2])
        turned = jnp.dot(pick, flat, preferred_element_type=jnp.float32).astype(coeffs.dtype)
        rows = [turned[t * senders : (t + 1) * senders] for t in range(step)]
    else:
        rows = [coeffs[:, t, :] for t in range(step)]
    for t in range(step):
        row = jnp.concatenate([rows[t][:, n * length : (n + 1) * length] for n in range(pieces)], axis=0)
        allowed = at[3 + first + t] >= orders[...]
        masked = jnp.where(allowed, row, jnp.zeros((), row.dtype))
        response = responses[t * slices // step][t % (step // slices)]
        back = lax.dot_general(response, masked, (((1,), (1,)), ((), ())), preferred_element_type=jnp.float32)
        back = back.astype(coeffs.dtype)
        part = width // fold
        for d in range(groups):
            parts = [back[d * width + h * part : d * width + (h + 1) * part] for h in range(fold)]
            outs[d][t] = parts[0] if fold == 1 else jnp.concatenate(parts, axis=1)


def folding(columns):
    return LANES // columns if columns < LANES and LANES % columns == 0 else 1


def radial_transform(at, blocks, orders, response, groups):
    near, rows, lanes = blocks[0].shape
    far = len(blocks)
    length = response.shape[1]
    columns = orders.shape[0]
    fold = folding(columns)
    shape = (length // groups // fold, columns * fold)
    step = 8 if rows % 8 == 0 else rows
    slices = math.gcd(step, 4)
    grid_spec = pltpu.PrefetchScalarGridSpec(
        num_scalar_prefetch=1,
        grid=(rows // step,),
        in_specs=[pl.BlockSpec((near, step, lanes), lambda t, at: (0, t, 0))] * far
        + [
            pl.BlockSpec((columns, 1), lambda t, at: (0, 0)),
        ]
        + [
            pl.BlockSpec((step // slices, length, length), lambda t, at, q=q: (t * slices + q, 0, 0))
            for q in range(slices)
        ],
        out_specs=[pl.BlockSpec((step, *shape), lambda t, at: (t, 0, 0))] * groups,
        scratch_shapes=[
            pltpu.VMEM((far * near if far > 1 else 1, step, lanes), jnp.bfloat16),
        ],
    )
    return pl.pallas_call(
        functools.partial(radial_kernel, groups, far, step, slices),
        grid_spec=grid_spec,
        out_shape=[jax.ShapeDtypeStruct((rows, *shape), jnp.bfloat16)] * groups,
        compiler_params=pltpu.CompilerParams(vmem_limit_bytes=VMEM),
        cost_estimate=pl.CostEstimate(
            flops=2 * rows * columns * length * length,
            bytes_accessed=2 * rows * (length * length + 2 * columns * length),
            transcendentals=0,
        ),
        name="radial",
    )(at, *blocks, orders, *[response] * slices)


def order_kernel(pieces, step, me, *refs):
    ins, place, out = refs[:pieces], refs[pieces], refs[-1]
    runs = place.shape[0]
    part = out.shape[1] // runs
    for h in range(runs):
        rows = []
        for t in range(step):
            rows.append(
                jnp.concatenate([p[t] if p.shape[1] == part else p[t, h * part : (h + 1) * part] for p in ins], axis=1)
            )
        mixed = jnp.dot(jnp.concatenate(rows, axis=0), place[h], preferred_element_type=jnp.float32)
        for t in range(step):
            out[t, h * part : (h + 1) * part] = mixed[t * part : (t + 1) * part].astype(out.dtype)


def placement(columns_of, total):
    runs = max(folding(columns.size) for columns in columns_of)
    matrices = []
    for h in range(runs):
        blocks = []
        for columns in columns_of:
            fold = folding(columns.size)
            block = (columns[:, None] == np.arange(total)[None, :]).astype(np.float32)
            blocks += [block if fold == 1 or k == h else 0 * block for k in range(fold)]
        matrices.append(np.concatenate(blocks))
    return jnp.asarray(np.stack(matrices), jnp.bfloat16)


def put_in_order(me, pieces, place, distance, so_far, groups, width):
    rows = pieces[0].shape[0]
    columns = place.shape[2]
    step = 8 if rows % 8 == 0 else rows
    specs = [pl.BlockSpec((step, *p.shape[1:]), lambda t, me: (t, 0, 0)) for p in pieces]
    specs.append(pl.BlockSpec(place.shape, lambda t, me: (0, 0, 0)))
    operands = list(pieces) + [place]
    aliases = {}
    if so_far is not None:
        specs.append(pl.BlockSpec(memory_space=pl.ANY))
        operands.append(so_far)
        aliases = {len(operands): 0}
    grid_spec = pltpu.PrefetchScalarGridSpec(
        num_scalar_prefetch=1,
        grid=(rows // step,),
        in_specs=specs,
        out_specs=pl.BlockSpec((step, width, columns), lambda t, me: ((me[0] ^ distance) * (rows // step) + t, 0, 0)),
    )
    return pl.pallas_call(
        functools.partial(order_kernel, len(pieces), step),
        grid_spec=grid_spec,
        out_shape=jax.ShapeDtypeStruct((groups * rows, width, columns), jnp.bfloat16),
        input_output_aliases=aliases,
        compiler_params=pltpu.CompilerParams(vmem_limit_bytes=VMEM),
        cost_estimate=pl.CostEstimate(
            flops=2 * rows * width * columns * place.shape[1], bytes_accessed=4 * rows * width * columns, transcendentals=0
        ),
        name="in_order",
    )(me, *operands)


def pack_kernel(*refs):
    xs, pick, out = refs[:-2], refs[-2], refs[-1]
    here = xs[0].shape[0] * len(xs)
    shell_blocks, sharers, _, columns = out.shape[:4]
    depth = xs[0].shape[2] * HALF
    for g in range(0, here, 2 * HALF):
        x, start = xs[g * len(xs) // here], g % (here // len(xs))
        found = [
            jnp.dot(
                pick[...],
                x[start + h : start + h + HALF, 0].reshape(depth, x.shape[3]),
                preferred_element_type=jnp.float32,
            )
            for h in (0, HALF)
        ]
        for n in range(shell_blocks * sharers * columns):
            rows = jnp.concatenate([f[n * HALF : (n + 1) * HALF] for f in found], axis=0)
            block, rest = divmod(n, sharers * columns)
            out[block, rest // columns, 0, rest % columns, 0, g : g + 2 * HALF] = rows.astype(out.dtype)


def pack(x, span, shells, sharers, spread):
    here, complex_parts, orders, cycles = x.shape
    lo, hi = span
    columns, parts = hi - lo, complex_parts // spread
    local = orders // shells
    per_device = local // sharers
    together = 2 * HALF // math.gcd(local, 2 * HALF)
    block, sharer, column, row = np.ix_(range(together), range(sharers), range(lo, hi), range(HALF))
    source = (row * together * local + block * local + sharer * per_device + column).reshape(-1, 1)
    pick = jnp.asarray(source == np.arange(HALF * together * local), jnp.bfloat16)
    shape = (shells, sharers, spread, columns, parts, here, cycles)
    slices = math.gcd(here // (2 * HALF), 4)
    return pl.pallas_call(
        pack_kernel,
        grid=(shells // together, complex_parts),
        in_specs=[
            *[
                pl.BlockSpec((here // slices, 1, together * local, cycles), lambda b, c, q=q: (q, c, b, 0))
                for q in range(slices)
            ],
            pl.BlockSpec(pick.shape, lambda b, c: (0, 0)),
        ],
        out_specs=pl.BlockSpec(
            (together, sharers, 1, columns, 1, here, cycles), lambda b, c: (b, 0, c // parts, 0, c % parts, 0, 0)
        ),
        out_shape=jax.ShapeDtypeStruct(shape, jnp.bfloat16),
        compiler_params=pltpu.CompilerParams(vmem_limit_bytes=VMEM),
        cost_estimate=pl.CostEstimate(
            flops=2 * pick.size * cycles * here // HALF * complex_parts * shells // together,
            bytes_accessed=2 * x.size + 2 * math.prod(shape),
            transcendentals=0,
        ),
        name="pack",
    )(*[x] * slices, pick)


def body(cycle_fourier, legendre, azimuth_orders, multipole, bessel, signal_power, noise_power):
    far, groups = lax.axis_size("far"), lax.axis_size("blk")
    shells = far * lax.axis_size("x")
    devices = shells * groups
    near = devices // far
    here, complex_parts, orders, cycles = cycle_fourier.shape
    local_orders, rows, _ = legendre.shape
    local_rows = multipole.shape[0]
    sharers = math.gcd(local_orders, groups)
    spread = groups // sharers
    per_device = local_orders // sharers
    parts = complex_parts // spread
    me = lax.axis_index("blk").astype(jnp.int32)
    indices = [lax.axis_index(name).astype(jnp.int32).reshape(1) for name in ("blk", NEAR, "far")]
    at = jnp.concatenate(indices + [multipole])

    cuts = [round(per_device * share / FIELD_SHARES[-1]) for share in FIELD_SHARES]
    spans = [(lo, hi) for lo, hi in zip(cuts, cuts[1:]) if hi > lo]
    cuts = [round(per_device * share / SHARES[-1]) for share in SHARES]
    chunks = [(lo, hi) for lo, hi in zip(cuts, cuts[1:]) if hi > lo]

    def packed(span):
        blocks = pack(cycle_fourier, span, shells, sharers, spread)
        return blocks.reshape(devices, span[1] - span[0], parts * here, cycles)

    def move(x, axes):
        return lax.all_to_all(x, axes, split_axis=0, concat_axis=0, tiled=True)

    def send_tables(span, earlier):
        lo, hi = span
        blocks = [
            lax.dynamic_slice_in_dim(legendre, (me ^ d) // spread * per_device + lo, hi - lo, 0) for d in range(1, groups)
        ]
        return exchange([None] + after(earlier, blocks), "blk", groups)[1:]

    def after(earlier, later):
        return lax.optimization_barrier((earlier, later))[1]

    order_view = azimuth_orders.reshape(shells, sharers, 1, per_device, 1)
    column_view = np.arange(orders * complex_parts).reshape(shells, sharers, per_device, spread, parts)
    limits, places = [], []
    for lo, hi in chunks:
        limit = jnp.broadcast_to(order_view[:, :, :, lo:hi], (shells, sharers, spread, hi - lo, parts))
        limits.append(limit.transpose(3, 4, 0, 1, 2).reshape(-1, 1))
        places.append(column_view[:, :, lo:hi].transpose(2, 4, 0, 1, 3).reshape(-1))
    place = placement(places, orders * complex_parts)
    response = radial_filter(at, bessel, signal_power[:, None, :], noise_power[:, None, :], groups)

    def coefficients(k, by_distance=False):
        lo, hi = chunks[k]
        which = max(i for i, span in enumerate(spans) if span[0] <= lo)
        start = spans[which][0]
        source = fields[which].reshape(shells, groups, *fields[which].shape[1:])
        sent = legendre_transform(
            at,
            legendre,
            tables[which],
            source,
            (start, lo - start),
            hi - lo,
            per_device,
            spread,
            parts,
            near if by_distance else devices,
            by_distance,
        )
        return sent if by_distance else sent.reshape(devices, local_rows, -1)

    fields = [move(packed(spans[0]), ALL)]
    tables = [send_tables(spans[0], ())]
    late, _ = lax.optimization_barrier((packed(spans[1]), (fields, tables, response, limits)))
    fields.append(move(late, ALL))
    first = coefficients(0, True)
    blocks = exchange([first[d] for d in range(near)], NEAR, near)
    tables.append(send_tables(spans[1], (fields[0], blocks)))
    arrived = exchange(regroup(at, blocks), "far", far)
    count = len(chunks)
    sent = [coefficients(k) for k in range(1, count)]
    ready = [x for x, chunk in zip(sent, chunks[1:]) if chunk[0] < spans[0][1]]
    before = [arrived, fields, tables, ready]
    outs, gathered = [], []
    for k in range(count):
        if k + 1 < count:
            coming = move(after(before, sent[k]), ALL)
        elif k >= 1:
            arrived = after((outs[k - 1], gathered[: k - 1]), arrived)
        outs.append(radial_transform(at, arrived, limits[k], response, groups))
        gathered.append(exchange(outs[k], "blk", groups))
        arrived = [coming]
        before = [coming, sent, gathered[k]]

    out = None
    for d in range(groups):
        out = put_in_order(at, [g[d] for g in gathered], place, d, out, groups, shells * here // groups)
    return out


def solution(mesh):
    shells, groups = mesh.shape["shell"], mesh.shape["blk"]
    far = 1 << shells.bit_length() // 2
    split = Mesh(mesh.devices.reshape(far, shells // far, groups), ALL)
    rows = P(ALL)
    return jax.shard_map(
        body,
        mesh=split,
        in_specs=(P(SHELL, None, None, "blk"), P(SHELL, None, "blk"), P(), rows, rows, rows, rows),
        out_specs=P(SHELL, "blk", None),
        check_vma=False,
    )
```

```python
import functools
import math

import jax
import jax.numpy as jnp
import numpy as np
from jax import lax
from jax.experimental import pallas as pl
from jax.experimental.pallas import tpu as pltpu
from jax.sharding import Mesh
from jax.sharding import PartitionSpec as P

LANES = 128
HALF = 8
NEAR = ("x", "blk")
SHELL = ("far", "x")
ALL = ("far", "x", "blk")
FIELD_SHARES = (0, 3, 6)
SHARES = (0, 1, 3, 5, 6)
VMEM = 48 * 1024 * 1024


def exchange(blocks, axis, size):
    return [blocks[0]] + [
        lax.ppermute(blocks[d], axis, [(i, i ^ d) for i in range(size)]) for d in range(1, size)
    ]


def legendre_kernel(groups, parts, by_distance, at, own, *refs):
    tables, fields, out = refs[: groups - 1], refs[groups - 1], refs[groups]
    lhs = jnp.concatenate([own[0]] + [t[0] for t in tables], axis=1)
    shells = fields.shape[0]
    height = fields.shape[3] // parts
    near, far, local_rows, _ = out.shape
    width = shells * height
    for c in range(parts):
        rows = [
            jnp.concatenate(
                [fields[s, at[0] ^ d, 0, c * height : (c + 1) * height] for d in range(groups)], axis=1
            )
            for s in range(shells)
        ]
        rhs = jnp.concatenate(rows, axis=0)
        total = lax.dot_general(lhs, rhs, (((1,), (1,)), ((), ())), preferred_element_type=jnp.float32)
        for i in range(far * near):
            device = i % near
            piece = total[i * local_rows : (i + 1) * local_rows].astype(out.dtype)
            out[device ^ at[1] if by_distance else device, i // near, :, c * width : (c + 1) * width] = piece


def legendre_transform(at, own, tables, fields, first, count, per_device, spread, parts, near, by_distance):
    shells, groups, _, height, cycles = fields.shape
    rows = own.shape[1]
    start, offset = first
    width = shells * height
    far = at_far(shells, groups, near)
    local_rows = rows // (near * far)
    grid_spec = pltpu.PrefetchScalarGridSpec(
        num_scalar_prefetch=1,
        grid=(count,),
        in_specs=[
            pl.BlockSpec((1, rows, cycles), lambda u, at: (at[0] // spread * per_device + start + offset + u, 0, 0))
        ]
        + [pl.BlockSpec((1, rows, cycles), lambda u, at: (offset + u, 0, 0))] * (groups - 1)
        + [pl.BlockSpec((shells, groups, 1, height, cycles), lambda u, at: (0, 0, offset + u, 0, 0))],
        out_specs=pl.BlockSpec((near, far, local_rows, width), lambda u, at: (0, 0, 0, u)),
    )
    flops = 2 * count * rows * width * cycles * groups
    return pl.pallas_call(
        functools.partial(legendre_kernel, groups, parts, by_distance),
        grid_spec=grid_spec,
        out_shape=jax.ShapeDtypeStruct((near, far, local_rows, count * width), jnp.bfloat16),
        compiler_params=pltpu.CompilerParams(vmem_limit_bytes=VMEM),
        cost_estimate=pl.CostEstimate(
            flops=flops, bytes_accessed=2 * count * (rows * width + groups * cycles * (rows + width)), transcendentals=0
        ),
        name="legendre",
    )(at, own, *tables, fields)


def at_far(shells, groups, near):
    return shells * groups // near


def regroup_kernel(count, at, *refs):
    ins, outs = refs[:count], refs[count:]
    for e, out in enumerate(outs):
        for d in range(count):
            out[at[1] ^ d] = ins[d][at[2] ^ e]


def regroup(at, blocks):
    near = len(blocks)
    far, rows, columns = blocks[0].shape
    lanes = columns // 2 if columns % (2 * LANES) == 0 else columns
    specs = [pl.BlockSpec((far, rows, lanes), lambda t, at: (0, 0, t))] * near
    return pl.pallas_call(
        functools.partial(regroup_kernel, len(blocks)),
        grid_spec=pltpu.PrefetchScalarGridSpec(
            num_scalar_prefetch=1,
            grid=(columns // lanes,),
            in_specs=specs,
            out_specs=[pl.BlockSpec((near, rows, lanes), lambda t, at: (0, 0, t))] * far,
        ),
        out_shape=[jax.ShapeDtypeStruct((near, rows, columns), jnp.bfloat16)] * far,
        compiler_params=pltpu.CompilerParams(vmem_limit_bytes=VMEM),
        cost_estimate=pl.CostEstimate(flops=0, bytes_accessed=4 * near * far * rows * columns, transcendentals=0),
        name="regroup",
    )(at, *blocks)


def filter_kernel(groups, at, bessel, signal, noise, out, held):
    for t in range(bessel.shape[0]):
        wiener = signal[t] / (signal[t] + noise[t])
        turned = (bessel[t].astype(jnp.float32).T * wiener).astype(jnp.bfloat16)
        response = jnp.dot(turned, bessel[t], preferred_element_type=jnp.float32).astype(out.dtype)
        width = response.shape[0] // groups
        for b in range(groups):
            held[b] = response[b * width : (b + 1) * width]
        for d in range(groups):
            out[t, d * width : (d + 1) * width] = held[at[0] ^ d]


def radial_filter(at, bessel, signal, noise, groups):
    rows, waves, shells = bessel.shape
    return pl.pallas_call(
        functools.partial(filter_kernel, groups),
        grid_spec=pltpu.PrefetchScalarGridSpec(
            num_scalar_prefetch=1,
            grid=(rows,),
            in_specs=[
                pl.BlockSpec((1, waves, shells), lambda t, at: (t, 0, 0)),
                pl.BlockSpec((1, 1, waves), lambda t, at: (t, 0, 0)),
                pl.BlockSpec((1, 1, waves), lambda t, at: (t, 0, 0)),
            ],
            out_specs=pl.BlockSpec((1, shells, shells), lambda t, at: (t, 0, 0)),
            scratch_shapes=[pltpu.VMEM((groups, shells // groups, shells), jnp.bfloat16)],
        ),
        out_shape=jax.ShapeDtypeStruct((rows, shells, shells), jnp.bfloat16),
        compiler_params=pltpu.CompilerParams(vmem_limit_bytes=VMEM),
        cost_estimate=pl.CostEstimate(
            flops=2 * rows * waves * shells * shells, bytes_accessed=4 * rows * shells * waves, transcendentals=0
        ),
        name="radial_filter",
    )(at, bessel, signal, noise)


def radial_kernel(groups, far, step, slices, at, *refs):
    ins, orders, responses = refs[:far], refs[far], refs[far + 1 : far + 1 + slices]
    outs, coeffs = refs[far + 1 + slices : -1], refs[-1]
    near = ins[0].shape[0]
    if far == 1:
        coeffs = ins[0]
    else:
        for e in range(far):
            coeffs[pl.ds((at[2] ^ e) * near, near)] = ins[e][...]
    first = pl.program_id(0) * step
    length = responses[0].shape[1]
    width = length // groups
    columns = orders.shape[0]
    fold = outs[0].shape[2] // columns
    senders = near * far
    pieces = coeffs.shape[2] // length
    if step % HALF == 0:
        size = senders * step
        to = lax.broadcasted_iota(jnp.int32, (size, size), 0)
        source = lax.broadcasted_iota(jnp.int32, (size, size), 1)
        pick = jnp.where(source == to % senders * step + to // senders, 1.0, 0.0).astype(coeffs.dtype)
        flat = coeffs[...].reshape(size, coeffs.shape[2])
        turned = jnp.dot(pick, flat, preferred_element_type=jnp.float32).astype(coeffs.dtype)
        rows = [turned[t * senders : (t + 1) * senders] for t in range(step)]
    else:
        rows = [coeffs[:, t, :] for t in range(step)]
    for t in range(step):
        row = jnp.concatenate([rows[t][:, n * length : (n + 1) * length] for n in range(pieces)], axis=0)
        allowed = at[3 + first + t] >= orders[...]
        masked = jnp.where(allowed, row, jnp.zeros((), row.dtype))
        response = responses[t * slices // step][t % (step // slices)]
        back = lax.dot_general(response, masked, (((1,), (1,)), ((), ())), preferred_element_type=jnp.float32)
        back = back.astype(coeffs.dtype)
        part = width // fold
        for d in range(groups):
            parts = [back[d * width + h * part : d * width + (h + 1) * part] for h in range(fold)]
            outs[d][t] = parts[0] if fold == 1 else jnp.concatenate(parts, axis=1)


def folding(columns):
    return LANES // columns if columns < LANES and LANES % columns == 0 else 1


def radial_transform(at, blocks, orders, response, groups):
    near, rows, lanes = blocks[0].shape
    far = len(blocks)
    length = response.shape[1]
    columns = orders.shape[0]
    fold = folding(columns)
    shape = (length // groups // fold, columns * fold)
    step = 8 if rows % 8 == 0 else rows
    slices = math.gcd(step, 4)
    grid_spec = pltpu.PrefetchScalarGridSpec(
        num_scalar_prefetch=1,
        grid=(rows // step,),
        in_specs=[pl.BlockSpec((near, step, lanes), lambda t, at: (0, t, 0))] * far
        + [
            pl.BlockSpec((columns, 1), lambda t, at: (0, 0)),
        ]
        + [
            pl.BlockSpec((step // slices, length, length), lambda t, at, q=q: (t * slices + q, 0, 0))
            for q in range(slices)
        ],
        out_specs=[pl.BlockSpec((step, *shape), lambda t, at: (t, 0, 0))] * groups,
        scratch_shapes=[
            pltpu.VMEM((far * near if far > 1 else 1, step, lanes), jnp.bfloat16),
        ],
    )
    return pl.pallas_call(
        functools.partial(radial_kernel, groups, far, step, slices),
        grid_spec=grid_spec,
        out_shape=[jax.ShapeDtypeStruct((rows, *shape), jnp.bfloat16)] * groups,
        compiler_params=pltpu.CompilerParams(vmem_limit_bytes=VMEM),
        cost_estimate=pl.CostEstimate(
            flops=2 * rows * columns * length * length,
            bytes_accessed=2 * rows * (length * length + 2 * columns * length),
            transcendentals=0,
        ),
        name="radial",
    )(at, *blocks, orders, *[response] * slices)


def order_kernel(pieces, step, me, *refs):
    ins, place, out = refs[:pieces], refs[pieces], refs[-1]
    runs = place.shape[0]
    part = out.shape[1] // runs
    for h in range(runs):
        rows = []
        for t in range(step):
            rows.append(
                jnp.concatenate([p[t] if p.shape[1] == part else p[t, h * part : (h + 1) * part] for p in ins], axis=1)
            )
        mixed = jnp.dot(jnp.concatenate(rows, axis=0), place[h], preferred_element_type=jnp.float32)
        for t in range(step):
            out[t, h * part : (h + 1) * part] = mixed[t * part : (t + 1) * part].astype(out.dtype)


def placement(columns_of, total):
    runs = max(folding(columns.size) for columns in columns_of)
    matrices = []
    for h in range(runs):
        blocks = []
        for columns in columns_of:
            fold = folding(columns.size)
            block = (columns[:, None] == np.arange(total)[None, :]).astype(np.float32)
            blocks += [block if fold == 1 or k == h else 0 * block for k in range(fold)]
        matrices.append(np.concatenate(blocks))
    return jnp.asarray(np.stack(matrices), jnp.bfloat16)


def put_in_order(me, pieces, place, distance, so_far, groups, width):
    rows = pieces[0].shape[0]
    columns = place.shape[2]
    step = rows // math.gcd(rows, 2)
    specs = [pl.BlockSpec((step, *p.shape[1:]), lambda t, me: (t, 0, 0)) for p in pieces]
    specs.append(pl.BlockSpec(place.shape, lambda t, me: (0, 0, 0)))
    operands = list(pieces) + [place]
    aliases = {}
    if so_far is not None:
        specs.append(pl.BlockSpec(memory_space=pl.ANY))
        operands.append(so_far)
        aliases = {len(operands): 0}
    grid_spec = pltpu.PrefetchScalarGridSpec(
        num_scalar_prefetch=1,
        grid=(rows // step,),
        in_specs=specs,
        out_specs=pl.BlockSpec((step, width, columns), lambda t, me: ((me[0] ^ distance) * (rows // step) + t, 0, 0)),
    )
    return pl.pallas_call(
        functools.partial(order_kernel, len(pieces), step),
        grid_spec=grid_spec,
        out_shape=jax.ShapeDtypeStruct((groups * rows, width, columns), jnp.bfloat16),
        input_output_aliases=aliases,
        compiler_params=pltpu.CompilerParams(vmem_limit_bytes=VMEM),
        cost_estimate=pl.CostEstimate(
            flops=2 * rows * width * columns * place.shape[1], bytes_accessed=4 * rows * width * columns, transcendentals=0
        ),
        name="in_order",
    )(me, *operands)


def pack_kernel(*refs):
    xs, pick, out = refs[:-2], refs[-2], refs[-1]
    here = xs[0].shape[0] * len(xs)
    shell_blocks, sharers, _, columns = out.shape[:4]
    depth = xs[0].shape[2] * HALF
    parts = out.shape[4]
    for c in range(xs[0].shape[1]):
        for g in range(0, here, 2 * HALF):
            x, start = xs[g * len(xs) // here], g % (here // len(xs))
            found = [
                jnp.dot(
                    pick[...],
                    x[start + h : start + h + HALF, c].reshape(depth, x.shape[3]),
                    preferred_element_type=jnp.float32,
                )
                for h in (0, HALF)
            ]
            for n in range(shell_blocks * sharers * columns):
                rows = jnp.concatenate([f[n * HALF : (n + 1) * HALF] for f in found], axis=0)
                block, rest = divmod(n, sharers * columns)
                out[block, rest // columns, c // parts, rest % columns, c % parts, g : g + 2 * HALF] = rows.astype(out.dtype)


def pack(x, span, shells, sharers, spread):
    here, complex_parts, orders, cycles = x.shape
    lo, hi = span
    columns, parts = hi - lo, complex_parts // spread
    local = orders // shells
    per_device = local // sharers
    together = 2 * HALF // math.gcd(local, 2 * HALF)
    block, sharer, column, row = np.ix_(range(together), range(sharers), range(lo, hi), range(HALF))
    source = (row * together * local + block * local + sharer * per_device + column).reshape(-1, 1)
    pick = jnp.asarray(source == np.arange(HALF * together * local), jnp.bfloat16)
    shape = (shells, sharers, spread, columns, parts, here, cycles)
    slices = math.gcd(here // (2 * HALF), 4)
    return pl.pallas_call(
        pack_kernel,
        grid=(shells // together,),
        in_specs=[
            *[
                pl.BlockSpec((here // slices, complex_parts, together * local, cycles), lambda b, q=q: (q, 0, b, 0))
                for q in range(slices)
            ],
            pl.BlockSpec(pick.shape, lambda b: (0, 0)),
        ],
        out_specs=pl.BlockSpec(
            (together, sharers, spread, columns, parts, here, cycles), lambda b: (b, 0, 0, 0, 0, 0, 0)
        ),
        out_shape=jax.ShapeDtypeStruct(shape, jnp.bfloat16),
        compiler_params=pltpu.CompilerParams(vmem_limit_bytes=VMEM),
        cost_estimate=pl.CostEstimate(
            flops=2 * pick.size * cycles * here // HALF * complex_parts * shells // together,
            bytes_accessed=2 * x.size + 2 * math.prod(shape),
            transcendentals=0,
        ),
        name="pack",
    )(*[x] * slices, pick)


def body(cycle_fourier, legendre, azimuth_orders, multipole, bessel, signal_power, noise_power):
    far, groups = lax.axis_size("far"), lax.axis_size("blk")
    shells = far * lax.axis_size("x")
    devices = shells * groups
    near = devices // far
    here, complex_parts, orders, cycles = cycle_fourier.shape
    local_orders, rows, _ = legendre.shape
    local_rows = multipole.shape[0]
    sharers = math.gcd(local_orders, groups)
    spread = groups // sharers
    per_device = local_orders // sharers
    parts = complex_parts // spread
    me = lax.axis_index("blk").astype(jnp.int32)
    indices = [lax.axis_index(name).astype(jnp.int32).reshape(1) for name in ("blk", NEAR, "far")]
    at = jnp.concatenate(indices + [multipole])

    cuts = [round(per_device * share / FIELD_SHARES[-1]) for share in FIELD_SHARES]
    spans = [(lo, hi) for lo, hi in zip(cuts, cuts[1:]) if hi > lo]
    cuts = [round(per_device * share / SHARES[-1]) for share in SHARES]
    chunks = [(lo, hi) for lo, hi in zip(cuts, cuts[1:]) if hi > lo]

    def packed(span):
        blocks = pack(cycle_fourier, span, shells, sharers, spread)
        return blocks.reshape(devices, span[1] - span[0], parts * here, cycles)

    def move(x, axes):
        return lax.all_to_all(x, axes, split_axis=0, concat_axis=0, tiled=True)

    def send_tables(span, earlier):
        lo, hi = span
        blocks = [
            lax.dynamic_slice_in_dim(legendre, (me ^ d) // spread * per_device + lo, hi - lo, 0) for d in range(1, groups)
        ]
        return exchange([None] + after(earlier, blocks), "blk", groups)[1:]

    def after(earlier, later):
        return lax.optimization_barrier((earlier, later))[1]

    order_view = azimuth_orders.reshape(shells, sharers, 1, per_device, 1)
    column_view = np.arange(orders * complex_parts).reshape(shells, sharers, per_device, spread, parts)
    limits, places = [], []
    for lo, hi in chunks:
        limit = jnp.broadcast_to(order_view[:, :, :, lo:hi], (shells, sharers, spread, hi - lo, parts))
        limits.append(limit.transpose(3, 4, 0, 1, 2).reshape(-1, 1))
        places.append(column_view[:, :, lo:hi].transpose(2, 4, 0, 1, 3).reshape(-1))
    place = placement(places, orders * complex_parts)
    response = radial_filter(at, bessel, signal_power[:, None, :], noise_power[:, None, :], groups)

    def coefficients(k, by_distance=False):
        lo, hi = chunks[k]
        which = max(i for i, span in enumerate(spans) if span[0] <= lo)
        start = spans[which][0]
        source = fields[which].reshape(shells, groups, *fields[which].shape[1:])
        sent = legendre_transform(
            at,
            legendre,
            tables[which],
            source,
            (start, lo - start),
            hi - lo,
            per_device,
            spread,
            parts,
            near if by_distance else devices,
            by_distance,
        )
        return sent if by_distance else sent.reshape(devices, local_rows, -1)

    fields = [move(packed(spans[0]), ALL)]
    tables = [send_tables(spans[0], ())]
    late, _ = lax.optimization_barrier((packed(spans[1]), (fields, tables, response, limits)))
    fields.append(move(late, ALL))
    first = coefficients(0, True)
    blocks = exchange([first[d] for d in range(near)], NEAR, near)
    tables.append(send_tables(spans[1], (fields[0], blocks)))
    arrived = exchange(regroup(at, blocks), "far", far)
    count = len(chunks)
    sent = [coefficients(k) for k in range(1, count)]
    ready = [x for x, chunk in zip(sent, chunks[1:]) if chunk[0] < spans[0][1]]
    before = [arrived, fields, tables, ready]
    outs, gathered = [], []
    for k in range(count):
        if k + 1 < count:
            coming = move(after(before, sent[k]), ALL)
        elif k >= 1:
            arrived = after((outs[k - 1], gathered[: k - 1]), arrived)
        outs.append(radial_transform(at, arrived, limits[k], response, groups))
        gathered.append(exchange(outs[k], "blk", groups))
        arrived = [coming]
        before = [coming, sent, gathered[k]]

    out = None
    for d in range(groups):
        out = put_in_order(at, [g[d] for g in gathered], place, d, out, groups, shells * here // groups)
    return out


def solution(mesh):
    shells, groups = mesh.shape["shell"], mesh.shape["blk"]
    far = 1 << shells.bit_length() // 2
    split = Mesh(mesh.devices.reshape(far, shells // far, groups), ALL)
    rows = P(ALL)
    return jax.shard_map(
        body,
        mesh=split,
        in_specs=(P(SHELL, None, None, "blk"), P(SHELL, None, "blk"), P(), rows, rows, rows, rows),
        out_specs=P(SHELL, "blk", None),
        check_vma=False,
    )
```
